32 devices in a mesh: groups: 2 (over y), rows: 4 (over z), samp: 2 (over x), sub: 2 (over core).
Axes of the slice: x: 2, y: 2, z: 4, core: 2. Of those that a mesh axis runs over, the one named last changes fastest.
Arguments:
- points: bfloat16 [131072, 256], P(('groups', 'rows', 'samp', 'sub')), parts along dimension 0, may hold values from -6 to 6
- inv_scale: float32 [512], P('groups'), parts along dimension 0, may hold values from 0.6 to 1.8
- labels: int32 [131072, 1], P(('groups', 'rows', 'samp', 'sub')), parts along dimension 0, may hold values from 0 to 3; in each aligned block of 4096 rows (0 to 4095, 4096 to 8191, ...) at most 2048 rows name the same one
- pattern: int32 [4, 1024], P(None, ('groups', 'rows', 'samp', 'sub')), parts along dimension 1, may hold values 0 or 1
- old_bases: bfloat16 [8, 32, 256], P(('groups', 'rows')), parts along dimension 0, may hold values from -0.375 to 0.375
Outputs:
- errors: float32 [4, 131072], P(None, ('groups', 'rows', 'samp', 'sub')), parts along dimension 1
- new_means: float32 [8, 256], P(('groups', 'rows')), parts along dimension 0
- new_bases: float32 [8, 32, 256], P(('groups', 'rows')), parts along dimension 0
The draws below stay inside these ranges and needn't reach their ends.
There are 2 independent parts, one for each index of `groups`. The reference program is written for one: setup_inputs(seed, part) draws one part's arguments, and reference() takes and returns one part's arrays. A program takes and returns all parts, laid end to end along the dimension named above; each array names one. Nothing has to cross between parts.
Inputs may be any that keep to these rules, and one draw needn't show every extreme that they name: `labels`: within the rows of one device no cluster is named more than 2048 times, and some cluster reaches 2048 in some devices; every cluster is named by some point.
All inputs are finite; a program needn't handle non-finite values. No bound on the sum of `pattern` on one device may be relied on, other than what follows from the above.
Results may differ from the reference program's by a relative error of at most 0.0029.
Values may be sent and summed in bfloat16 or wider, within the bound.
A program may use at most 64 MiB of HBM per device.

```python
import math
import jax
import jax.numpy as jnp
import numpy as np
from jax import lax

V = 256
R = 32
ROWS_DEV = 4096
TILE = 128
STEPS = 2
K = 4
POINTS = 65536
CAP = 2048
TILES = 512
N_ROWS = 4
N_SAMP = 2
N_SUB = 2


def place_ends(entries, rng, low, high):
    longest = entries.shape.index(max(entries.shape))
    spots = []
    for shift in (0, 1):
        where = [jax.random.randint(jax.random.fold_in(rng, axis), (), 0, length) for axis, length in enumerate(entries.shape)]
        where[longest] = (where[longest] + shift) % entries.shape[longest]
        spots.append(tuple(where))
    return entries.at[spots[0]].set(low).at[spots[1]].set(high)


def steps_of(key, extent, cuts, smallest, largest):
    def one(position, shards_of):
        heights = jax.random.uniform(jax.random.fold_in(jax.random.fold_in(key, 6), position), (shards_of,), jnp.float32, smallest / len(cuts), largest / len(cuts))
        return jnp.repeat(jnp.exp(heights), extent[position] // shards_of).reshape((-1,) + (1,) * (len(extent) - position - 1))

    loudness = one(*cuts[0])
    for cut in cuts[1:]:
        loudness = loudness * one(*cut)
    return loudness


def deal_out(key, own, number, rows, count, top, most, skew):
    sequence = jax.random.permutation(key, count)
    packed, ordinary = portions_of(count, rows * top, most, skew, True), portions_of(count, rows * top, most, skew, False)
    places = jnp.arange(count)

    def named(tallies, rotation):
        used = int((tallies > 0).sum())
        fixed = max(1, used // 4)
        moved = fixed + (places - fixed + rotation * (used - fixed)) % max(1, count - fixed)
        return jnp.zeros((count,), jnp.int32).at[sequence[jnp.where(places < fixed, places, moved)]].set(jnp.asarray(tallies, jnp.int32))

    tallies = jnp.where(number % 4 == 0, named(packed, number // 4), named(ordinary, number - number // 4 - 1))
    mixed = jax.random.permutation(jax.random.fold_in(own, 3), count)
    source_of, taker = mixed[0:count // 2 * 2:2], mixed[1:count // 2 * 2:2]
    margin = jnp.minimum(tallies[source_of] - 1, most - tallies[taker]) // 2
    margin = jnp.where((source_of == sequence[0]) | (taker == sequence[0]) | (tallies[taker] == 0), 0, jnp.maximum(margin, 0))
    moved = jax.random.randint(jax.random.fold_in(own, 4), (count // 2,), 0, 1 << 20) % (margin + 1)
    tallies = tallies.at[source_of].add(-moved).at[taker].add(moved)
    items = jnp.searchsorted(jnp.cumsum(tallies), jnp.arange(rows * top), side="right").astype(jnp.int32)
    listing = items.reshape(top, rows).T
    listing = listing[jax.random.permutation(jax.random.fold_in(own, 1), rows)]
    rotation = jax.random.randint(jax.random.fold_in(own, 2), (rows, 1), 0, top)
    return jnp.take_along_axis(listing, (jnp.arange(top)[None, :] + rotation) % top, axis=1)


def portions_of(number_of, total, limit, slope, full):
    portions = [(1 << 20) // math.isqrt(grade ** slope) + 1 for grade in range(1, number_of + 1)]
    largest = limit if full else min(limit, max(-(-total // number_of), total * portions[0] // sum(portions)))
    least = 1 if total - largest >= number_of - 1 else 0
    given, spare = [largest] + [least] * (number_of - 1), total - largest - least * (number_of - 1)
    while spare > 0:
        candidates = [i for i in range(1, number_of) if given[i] < largest] or [i for i in range(1, number_of) if given[i] < limit]
        whole, remaining = sum([portions[i] for i in candidates]), spare
        for i in candidates:
            extra = min(limit - given[i], max(1, remaining * portions[i] // whole), spare)
            given[i] = given[i] + extra
            spare = spare - extra
    return np.array(given)


def bell_draw(own_key, shape, deviation, most, cuts=(), kind=jnp.bfloat16):
    factor_of = steps_of(own_key, shape, cuts, -0.22, 0.18) if cuts else 1.0
    drawn = jax.random.normal(own_key, shape, jnp.float32) * deviation * factor_of
    return jnp.minimum(jnp.maximum(drawn, -most), most).astype(kind)


def setup_inputs(seed: int = 0, part: int = 0) -> dict:
    keys = jax.random.split(jax.random.key(seed), 6)
    part_keys = jax.random.split(jax.random.fold_in(keys[5], part), 6)
    points = bell_draw(part_keys[0], (POINTS, V), 1.0, 6.0, ((0, 16),))
    inv_scale = jnp.clip(jnp.exp(jax.random.uniform(part_keys[1], (V,), jnp.float32, math.log(0.6), math.log(1.8))), 0.6, 1.8)
    labels_keys = jax.random.split(jax.random.fold_in(part_keys[2], 1), POINTS // ROWS_DEV)
    labels_turns = jax.random.permutation(jax.random.fold_in(part_keys[2], 3), POINTS // ROWS_DEV)
    labels = jax.vmap(lambda own, number: deal_out(jax.random.fold_in(part_keys[2], 2), own, number, ROWS_DEV, K, 1, CAP, 2))(labels_keys, labels_turns).reshape((POINTS, 1))
    pattern = place_ends((jax.random.randint(part_keys[3], (K, TILES), 0, 2) < 1).astype(jnp.int32), jax.random.fold_in(part_keys[3], 1), 0, 1)
    old_bases = bell_draw(part_keys[4], (K, R, V), V ** -0.5, 0.375, ((0, 4),))
    return {"points": points, "inv_scale": inv_scale, "labels": labels, "pattern": pattern, "old_bases": old_bases}


def arrange(scaled, label_ids, clusters, capacity):
    features = scaled.shape[1]
    member = (label_ids[:, None] == jnp.arange(clusters, dtype=jnp.int32)[None, :]).astype(jnp.int32)
    ranking = jnp.sum((jnp.cumsum(member, axis=0) - 1) * member, axis=1).astype(jnp.int32)
    target = (label_ids * capacity + ranking).astype(jnp.int32)
    buffer = jnp.zeros((clusters * capacity, features), scaled.dtype).at[target].set(scaled)
    return buffer.reshape(clusters, capacity, features)

def refine(subspace, covariance):
    for iteration in range(STEPS):
        mapped = jnp.dot(subspace, covariance, precision=lax.Precision.HIGHEST)
        correlation = jnp.dot(mapped, mapped.T, precision=lax.Precision.HIGHEST)
        factor = jnp.linalg.cholesky(correlation)
        subspace = jax.scipy.linalg.solve_triangular(factor, mapped, lower=True)
    return subspace

def cluster_errors(scaled, row_mask, centers, bases_low):
    clusters, rank_count, features = bases_low.shape
    flat = bases_low.reshape(clusters * rank_count, features)
    shift = jnp.einsum('nrv,nv->nr', bases_low.astype(jnp.float32), centers, precision=lax.Precision.HIGHEST)
    center_sq = jnp.sum(centers * centers, axis=1)
    rows_total = scaled.shape[0]
    span = min(1024, rows_total)
    stacked = scaled.reshape(rows_total // span, span, features)

    def one_block(row_block):
        projected = lax.dot_general(row_block.astype(jnp.float32), flat.astype(jnp.float32), (((1,), (1,)), ((), ())), preferred_element_type=jnp.float32)
        projected = projected.reshape(span, clusters, rank_count) - shift[None]
        widened = row_block.astype(jnp.float32)
        cross = jnp.dot(widened, centers.T, precision=lax.Precision.HIGHEST)
        distance = jnp.sum(widened * widened, axis=1)[:, None] - 2.0 * cross + center_sq[None, :]
        return (distance - jnp.sum(projected * projected, axis=2)) / features
    result = lax.map(one_block, stacked).reshape(rows_total, clusters)
    return result.T * row_mask

def reference(points, inv_scale, labels, pattern, old_bases):
    clusters = N_ROWS
    devices_all = N_ROWS * N_SAMP * N_SUB
    scaled = (points.astype(jnp.float32) * inv_scale[None, :]).astype(jnp.bfloat16)
    label_ids = labels[:, 0].astype(jnp.int32)
    counts = jax.ops.segment_sum(jnp.ones(label_ids.shape, jnp.float32), label_ids, num_segments=clusters)
    totals = jax.ops.segment_sum(scaled.astype(jnp.float32), label_ids, num_segments=clusters)
    centers = totals / counts[:, None]
    shards = scaled.reshape(devices_all, ROWS_DEV, V)
    label_shards = label_ids.reshape(devices_all, ROWS_DEV)

    def add_device(running, inputs):
        buffer = arrange(inputs[0], inputs[1], clusters, CAP).astype(jnp.float32)
        return (running + jnp.einsum('kcv,kcw->kvw', buffer, buffer, precision=lax.Precision.HIGHEST), None)
    grams, unused = lax.scan(add_device, jnp.zeros((clusters, V, V), jnp.float32), (shards, label_shards))
    covariance = grams / counts[:, None, None] - centers[:, :, None] * centers[:, None, :]
    subspace = jax.vmap(refine)(old_bases.astype(jnp.float32), covariance)
    sent = subspace.astype(jnp.bfloat16)
    row_mask = jnp.repeat(pattern.astype(jnp.float32), TILE, axis=1)
    mask_shards = row_mask.reshape(clusters, devices_all, ROWS_DEV).transpose(1, 0, 2)

    def device_errors(inputs):
        return cluster_errors(inputs[0], inputs[1], centers, sent)
    errors = lax.map(device_errors, (shards, mask_shards))
    errors = errors.transpose(1, 0, 2).reshape(clusters, POINTS)
    return (errors, centers, subspace)
```

```python
import functools

import jax
import jax.numpy as jnp
from jax import lax
from jax.experimental import pallas as pl
from jax.experimental.pallas import tpu as pltpu
from jax.sharding import PartitionSpec as P

TILE = 128
STEPS = 2
HALF = 128
F32 = jnp.float32
BF16 = jnp.bfloat16
HIGH = lax.Precision.HIGHEST
NT = (((1,), (1,)), ((), ()))


def round_up(value, unit):
    return -(-value // unit) * unit


def send(src, dst, send_sem, recv_sem, where):
    return pltpu.make_async_remote_copy(
        src_ref=src,
        dst_ref=dst,
        send_sem=send_sem,
        recv_sem=recv_sem,
        device_id=where,
        device_id_type=pl.DeviceIdType.MESH,
    )


def kernel(
    n_rows, n_samp, n_sub,
    points_ref, scale_ref, labels_ref, pattern_ref, old_ref,
    errors_ref, means_ref, bases_ref,
    scaled, flipped, packed, sub_in, half_sum, samp_in, reduced, rows_in, gathered,
    stat, stat_sub_in, stat_half, stat_samp_in, stat_rows, means, square, distance,
    cov, wide, sent,
    s_sub, r_sub, s_samp, r_samp, s_rows, r_rows, s_gat, r_gat,
    s_st_sub, r_st_sub, s_st_samp, r_st_samp, s_st_rows, r_st_rows, s_bas, r_bas,
):
    clusters = n_rows
    rows_total, features = points_ref.shape
    rank = old_ref.shape[0]
    half = 3 * HALF // n_sub
    piece = half // n_samp
    team = n_samp * n_sub
    row = lax.axis_index("rows")
    samp = lax.axis_index("samp")
    sub = lax.axis_index("sub")
    place = sub * n_samp + samp

    def mate(step):
        spot = lax.rem(place + step, team)
        return {"samp": lax.rem(spot, n_samp), "sub": lax.div(spot, n_samp)}

    def other(index, step, size):
        return lax.rem(index + step, size)

    barrier = pltpu.get_barrier_semaphore()
    for step in range(1, team):
        pl.semaphore_signal(barrier, inc=1, device_id=mate(step), device_id_type=pl.DeviceIdType.MESH)
    for step in range(1, n_rows):
        pl.semaphore_signal(
            barrier, inc=1, device_id={"rows": other(row, step, n_rows)},
            device_id_type=pl.DeviceIdType.MESH,
        )

    block = min(512, rows_total)
    for start in range(0, rows_total, block):
        span = slice(start, start + block)
        value = (points_ref[span, :].astype(F32) * scale_ref[...]).astype(BF16)
        scaled[span, :] = value
        turned = value.T
        flipped[:, span] = turned
        full = turned.astype(F32)
        square[:, span] = jnp.sum(full * full, axis=0, keepdims=True)

    padded = means.shape[0]
    labels = labels_ref[...]
    member = (
        lax.broadcasted_iota(jnp.int32, (padded, rows_total), 0) == labels
    ).astype(F32)
    sums = jnp.dot(member.astype(BF16), scaled[...], preferred_element_type=F32)
    counts = jnp.broadcast_to(jnp.sum(member, axis=1, keepdims=True), (padded, features))
    stat[0:clusters, :] = sums[0:clusters]
    stat[clusters : 2 * clusters, :] = counts[0:clusters]

    pl.semaphore_wait(barrier, team - 1 + n_rows - 1)
    sub_peer = {"sub": 1 - sub}

    def sub_copy(c):
        return send(
            packed.at[c, pl.ds(pl.multiple_of((1 - sub) * half, 8), half)],
            sub_in.at[c], s_sub.at[c], r_sub.at[c], sub_peer,
        )

    def samp_copy(c, step):
        peer = other(samp, step, n_samp)
        return send(
            half_sum.at[c, pl.ds(pl.multiple_of(peer * piece, 8), piece)],
            samp_in.at[c, step - 1], s_samp.at[c, step - 1], r_samp.at[c, step - 1],
            {"samp": peer},
        )

    def rows_copy(c, source):
        return send(
            reduced.at[c], rows_in.at[source], s_rows.at[c], r_rows.at[source], {"rows": c}
        )

    stat_sub = send(stat, stat_sub_in, s_st_sub, r_st_sub, sub_peer)
    stat_sub.start()
    stat_samp = [
        send(
            stat_half, stat_samp_in.at[samp], s_st_samp.at[step - 1], r_st_samp.at[step - 1],
            {"samp": other(samp, step, n_samp)},
        )
        for step in range(1, n_samp)
    ]
    stat_row = [
        send(
            stat_rows.at[row], stat_rows.at[row], s_st_rows.at[step - 1], r_st_rows.at[step - 1],
            {"rows": other(row, step, n_rows)},
        )
        for step in range(1, n_rows)
    ]

    def compute(c):
        mask = (labels == c).astype(F32).astype(BF16)
        gram = jnp.dot(flipped[...] * mask, scaled[...], preferred_element_type=F32)
        packed[c, 0:HALF, :] = gram[0:HALF, 0:HALF]
        packed[c, HALF : 2 * HALF, :] = gram[0:HALF, HALF:]
        packed[c, 2 * HALF :, :] = gram[HALF:, HALF:]
        sub_copy(c).start()

    def add_sub(c):
        sub_copy(c).wait_recv()
        half_sum[c] = packed[c, pl.ds(pl.multiple_of(sub * half, 8), half), :] + sub_in[c]
        for step in range(1, n_samp):
            samp_copy(c, step).start()

    def add_samp(c):
        for step in range(1, n_samp):
            samp_copy(c, step).wait_recv()
        total = half_sum[c, pl.ds(pl.multiple_of(samp * piece, 8), piece), :]
        for step in range(1, n_samp):
            total = total + samp_in[c, step - 1]
        reduced[c] = total

        @pl.when(row != c)
        def _():
            rows_copy(c, row).start()

    def stat_stage(stage):
        if stage == 1:
            stat_sub.wait_recv()
            stat_half[...] = stat[...] + stat_sub_in[...]
            for copy in stat_samp:
                copy.start()
            stat_samp_in[samp] = stat_half[...]
        if stage == 2:
            for copy in stat_samp:
                copy.wait_recv()
            total = stat_samp_in[0]
            for index in range(1, n_samp):
                total = total + stat_samp_in[index]
            stat_rows[row] = total
            for copy in stat_row:
                copy.start()
        if stage == 3:
            for copy in stat_row:
                copy.wait_recv()
            total = stat_rows[0]
            for index in range(1, n_rows):
                total = total + stat_rows[index]
            stat[...] = total

    for tick in range(clusters + 2):
        if tick < clusters:
            compute(tick)
        if tick == 1:
            stat_stage(1)
        if 0 <= tick - 1 < clusters:
            add_sub(tick - 1)
        if tick == 2:
            stat_stage(2)
        if 0 <= tick - 2 < clusters:
            add_samp(tick - 2)

    stat_sub.wait_send()
    stat_stage(3)
    centers = stat[0:clusters, :] / stat[clusters : 2 * clusters, :]
    means[...] = jnp.zeros_like(means)
    means[0:clusters, :] = centers
    own = means[pl.ds(row, 1), :]
    own_count = stat[pl.ds(clusters + row, 1), :]
    means_ref[...] = own
    every = means[...]
    top = every.astype(BF16)
    rest = every - top.astype(F32)
    middle = rest.astype(BF16)
    last = (rest - middle.astype(F32)).astype(BF16)
    parts = jnp.concatenate([top, middle, last], axis=0)
    norm = jnp.sum(every * every, axis=1, keepdims=True)
    for start in range(0, rows_total, block):
        span = slice(start, start + block)
        cross = lax.dot_general(parts, scaled[span, :], NT, preferred_element_type=F32)
        cross = cross[0:padded] + (cross[padded : 2 * padded] + cross[2 * padded :])
        distance[:, span] = square[:, span] - 2.0 * cross + norm

    total = reduced[row]
    for step in range(1, n_rows):
        source = other(row, step, n_rows)
        pltpu.make_async_remote_copy(
            src_ref=rows_in.at[source], dst_ref=rows_in.at[source],
            send_sem=s_rows.at[source], recv_sem=r_rows.at[source],
            device_id={"rows": source}, device_id_type=pl.DeviceIdType.MESH,
        ).wait_recv()
        total = total + rows_in[source]
    gathered[place] = total
    gather = [
        send(
            gathered.at[place], gathered.at[place], s_gat.at[step - 1], r_gat.at[step - 1],
            mate(step),
        )
        for step in range(1, team)
    ]
    for copy in gather:
        copy.start()
    wide[...] = jnp.zeros_like(wide)
    for copy in gather:
        copy.wait_recv()
    whole = gathered[...].reshape(3 * HALF, HALF)
    cov[0:HALF, 0:HALF] = whole[0:HALF]
    cov[0:HALF, HALF:] = whole[HALF : 2 * HALF]
    cov[HALF:, 0:HALF] = whole[HALF : 2 * HALF].T
    cov[HALF:, HALF:] = whole[2 * HALF :]

    basis = old_ref[...].astype(F32)
    inverse = 1.0 / own_count
    lane = lax.broadcasted_iota(jnp.int32, (rank, 128), 1)
    line = lax.broadcasted_iota(jnp.int32, (rank, 128), 0)
    for _ in range(STEPS):
        mapped = jnp.dot(basis, cov[...], precision=HIGH, preferred_element_type=F32) * inverse
        mapped = mapped - jnp.sum(basis * own, axis=1, keepdims=True) * own
        wide[rank : 2 * rank, :] = mapped
        table = lax.dot_general(
            mapped, wide[rank : rank + 128, :], NT, precision=HIGH, preferred_element_type=F32
        )
        table = jnp.where(lane == line + rank, 1.0, table)
        for j in range(rank):
            column = jnp.broadcast_to(table[:, j : j + 1], (rank, 128))
            pivot = table[j : j + 1, :] / column[j : j + 1, :]
            table = table - jnp.where(line > j, column, 0.0) * pivot
        diagonal = jnp.sum(jnp.where(lane == line, table, 0.0), axis=1, keepdims=True)
        table = jnp.where(lane < rank, 0.0, table * lax.rsqrt(diagonal))
        basis = jnp.dot(table, wide[0:128, :], precision=HIGH, preferred_element_type=F32)
    bases_ref[...] = basis
    sent[row] = basis.astype(BF16)
    spread = [
        send(
            sent.at[row], sent.at[row], s_bas.at[step - 1], r_bas.at[step - 1],
            {"rows": other(row, step, n_rows)},
        )
        for step in range(1, n_rows)
    ]
    for copy in spread:
        copy.start()
    for copy in spread:
        copy.wait_recv()

    flat = sent[...].reshape(clusters * rank, features)
    shift = [
        jnp.sum(sent[c].astype(F32) * means[c : c + 1, :], axis=1, keepdims=True)
        for c in range(clusters)
    ]
    for start in range(0, rows_total, block):
        span = slice(start, start + block)
        proj = lax.dot_general(flat, scaled[span, :], NT, preferred_element_type=F32)
        for c in range(clusters):
            part = proj[c * rank : (c + 1) * rank] - shift[c]
            value = distance[c : c + 1, span] - jnp.sum(part * part, axis=0, keepdims=True)
            mask = jnp.concatenate(
                [
                    jnp.broadcast_to(pattern_ref[c : c + 1, t : t + 1], (1, TILE))
                    for t in range(start // TILE, (start + block) // TILE)
                ],
                axis=1,
            )
            errors_ref[c : c + 1, span] = mask.astype(F32) * value / features

    for c in range(clusters):
        sub_copy(c).wait_send()
        for step in range(1, n_samp):
            samp_copy(c, step).wait_send()

        @pl.when(row != c)
        def _():
            rows_copy(c, row).wait_send()
    for copy in stat_samp + stat_row + gather + spread:
        copy.wait_send()


def shards(points, inv_scale, labels, pattern, old_bases):
    n_rows = lax.axis_size("rows")
    n_samp = lax.axis_size("samp")
    n_sub = lax.axis_size("sub")
    rows_total, features = points.shape
    rank = old_bases.shape[1]
    clusters = n_rows
    half = 3 * HALF // n_sub
    piece = half // n_samp
    team = n_samp * n_sub
    padded = round_up(clusters, 16)
    dma = pltpu.SemaphoreType.DMA
    vmem = pltpu.VMEM
    specs = pl.BlockSpec(memory_space=pltpu.VMEM)
    errors, centers, subspace = pl.pallas_call(
        functools.partial(kernel, n_rows, n_samp, n_sub),
        out_shape=(
            jax.ShapeDtypeStruct((clusters, rows_total), F32),
            jax.ShapeDtypeStruct((1, features), F32),
            jax.ShapeDtypeStruct((rank, features), F32),
        ),
        in_specs=[specs] * 5,
        out_specs=(specs,) * 3,
        scratch_shapes=[
            vmem((rows_total, features), BF16),
            vmem((features, rows_total), BF16),
            vmem((clusters, 3 * HALF, HALF), F32),
            vmem((clusters, half, HALF), F32),
            vmem((clusters, half, HALF), F32),
            vmem((clusters, n_samp - 1, piece, HALF), F32),
            vmem((clusters, piece, HALF), F32),
            vmem((n_rows, piece, HALF), F32),
            vmem((team, piece, HALF), F32),
            vmem((2 * clusters, features), F32),
            vmem((2 * clusters, features), F32),
            vmem((2 * clusters, features), F32),
            vmem((n_samp, 2 * clusters, features), F32),
            vmem((n_rows, 2 * clusters, features), F32),
            vmem((padded, features), F32),
            vmem((1, rows_total), F32),
            vmem((padded, rows_total), F32),
            vmem((features, features), F32),
            vmem((rank + 128, features), F32),
            vmem((n_rows, rank, features), BF16),
            dma((clusters,)), dma((clusters,)),
            dma((clusters, n_samp - 1)), dma((clusters, n_samp - 1)),
            dma((clusters,)), dma((n_rows,)),
            dma((team - 1,)), dma((team - 1,)),
            dma, dma,
            dma((n_samp - 1,)), dma((n_samp - 1,)),
            dma((n_rows - 1,)), dma((n_rows - 1,)),
            dma((n_rows - 1,)), dma((n_rows - 1,)),
        ],
        compiler_params=pltpu.CompilerParams(
            collective_id=0, has_side_effects=True, vmem_limit_bytes=48 * 1024 * 1024
        ),
    )(
        points,
        inv_scale.reshape(1, features),
        labels.reshape(1, rows_total),
        pattern,
        old_bases[0],
    )
    return (errors, centers, subspace[None])


def solution(mesh):
    return jax.shard_map(
        shards,
        mesh=mesh,
        in_specs=(
            P(("groups", "rows", "samp", "sub"), None),
            P("groups"),
            P(("groups", "rows", "samp", "sub"), None),
            P(None, ("groups", "rows", "samp", "sub")),
            P(("groups", "rows"), None, None),
        ),
        out_specs=(
            P(None, ("groups", "rows", "samp", "sub")),
            P(("groups", "rows"), None),
            P(("groups", "rows"), None, None),
        ),
        check_vma=False,
    )
```

```python
import functools

import jax
import jax.numpy as jnp
from jax import lax
from jax.experimental import pallas as pl
from jax.experimental.pallas import tpu as pltpu
from jax.sharding import PartitionSpec as P

TILE = 128
STEPS = 2
HALF = 128
GROUP = 8
F32 = jnp.float32
BF16 = jnp.bfloat16
HIGH = lax.Precision.HIGHEST
NT = (((1,), (1,)), ((), ()))


def round_up(value, unit):
    return -(-value // unit) * unit


def send(src, dst, send_sem, recv_sem, where):
    return pltpu.make_async_remote_copy(
        src_ref=src,
        dst_ref=dst,
        send_sem=send_sem,
        recv_sem=recv_sem,
        device_id=where,
        device_id_type=pl.DeviceIdType.MESH,
    )


def kernel(
    n_rows, n_samp, n_sub,
    points_hbm, scale_hbm, labels_hbm, pattern_hbm, old_hbm,
    errors_ref, means_ref, bases_ref,
    scaled, flipped, packed, sub_in, half_sum, samp_in, reduced, rows_in, gathered,
    stat, stat_sub_in, stat_half, stat_samp_in, stat_rows, means, square, distance,
    cov, wide, sent,
    points_ref, scale_ref, labels_ref, pattern_ref, old_ref, s_in, s_points,
    s_sub, r_sub, s_samp, r_samp, s_rows, r_rows, s_gat, r_gat,
    s_st_sub, r_st_sub, s_st_samp, r_st_samp, s_st_rows, r_st_rows, s_bas, r_bas,
):
    clusters = n_rows
    rows_total, features = points_ref.shape
    rank = old_ref.shape[0]
    half = 2 * HALF // n_sub
    piece = half // n_samp
    team = n_samp * n_sub
    row = lax.axis_index("rows")
    samp = lax.axis_index("samp")
    sub = lax.axis_index("sub")
    place = sub * n_samp + samp

    def mate(step):
        spot = lax.rem(place + step, team)
        return {"samp": lax.rem(spot, n_samp), "sub": lax.div(spot, n_samp)}

    def other(index, step, size):
        return lax.rem(index + step, size)

    barrier = pltpu.get_barrier_semaphore()
    for step in range(1, team):
        pl.semaphore_signal(barrier, inc=1, device_id=mate(step), device_id_type=pl.DeviceIdType.MESH)
    for step in range(1, n_rows):
        pl.semaphore_signal(
            barrier, inc=1, device_id={"rows": other(row, step, n_rows)},
            device_id_type=pl.DeviceIdType.MESH,
        )

    block = min(512, rows_total)
    loads = [
        pltpu.make_async_copy(
            points_hbm.at[start : start + block], points_ref.at[start : start + block],
            s_points.at[start // block],
        )
        for start in range(0, rows_total, block)
    ]
    extras = [
        pltpu.make_async_copy(source, target, s_in.at[index])
        for index, (source, target) in enumerate(
            (
                (scale_hbm, scale_ref),
                (labels_hbm, labels_ref),
                (pattern_hbm, pattern_ref),
                (old_hbm, old_ref),
            )
        )
    ]
    extras[0].start()
    loads[0].start()
    extras[1].start()
    for copy in loads[1:] + extras[2:]:
        copy.start()
    extras[0].wait()

    for start in range(0, rows_total, block):
        span = slice(start, start + block)
        loads[start // block].wait()
        value = (points_ref[span, :].astype(F32) * scale_ref[...]).astype(BF16)
        scaled[span, :] = value
        turned = value.T
        flipped[:, span] = turned
        full = turned.astype(F32)
        square[:, span] = jnp.sum(full * full, axis=0, keepdims=True)

    for copy in extras[1:]:
        copy.wait()
    padded = means.shape[0]
    labels = labels_ref[...]
    member = (
        lax.broadcasted_iota(jnp.int32, (padded, rows_total), 0) == labels
    ).astype(F32)
    sums = jnp.dot(member.astype(BF16), scaled[...], preferred_element_type=F32)
    counts = jnp.broadcast_to(jnp.sum(member, axis=1, keepdims=True), (padded, features))
    stat[0:clusters, :] = sums[0:clusters]
    stat[clusters : 2 * clusters, :] = counts[0:clusters]

    pl.semaphore_wait(barrier, team - 1 + n_rows - 1)
    sub_peer = {"sub": 1 - sub}

    def sub_copy(c):
        return send(
            packed.at[c, pl.ds(pl.multiple_of((1 - sub) * half, 8), half)],
            sub_in.at[c], s_sub.at[c], r_sub.at[c], sub_peer,
        )

    def samp_copy(c, step):
        peer = other(samp, step, n_samp)
        return send(
            half_sum.at[c, pl.ds(pl.multiple_of(peer * piece, 8), piece)],
            samp_in.at[c, step - 1], s_samp.at[c, step - 1], r_samp.at[c, step - 1],
            {"samp": peer},
        )

    def rows_copy(c, source):
        return send(
            reduced.at[c], rows_in.at[source], s_rows.at[c], r_rows.at[source], {"rows": c}
        )

    stat_sub = send(stat, stat_sub_in, s_st_sub, r_st_sub, sub_peer)
    stat_samp = [
        send(
            stat_half, stat_samp_in.at[samp], s_st_samp.at[step - 1], r_st_samp.at[step - 1],
            {"samp": other(samp, step, n_samp)},
        )
        for step in range(1, n_samp)
    ]
    stat_row = [
        send(
            stat_rows.at[row], stat_rows.at[row], s_st_rows.at[step - 1], r_st_rows.at[step - 1],
            {"rows": other(row, step, n_rows)},
        )
        for step in range(1, n_rows)
    ]

    down = lax.broadcasted_iota(jnp.int32, (HALF, HALF), 0)
    across = lax.broadcasted_iota(jnp.int32, (HALF, HALF), 1)

    def compute(c):
        mask = (labels == c).astype(F32).astype(BF16)
        gram = jnp.dot(flipped[...] * mask, scaled[...], preferred_element_type=F32)
        corner, opposite = gram[0:HALF, 0:HALF], gram[HALF:, HALF:]
        packed[c, 0:HALF, :] = jnp.where(across > down, corner, opposite)
        packed[c, HALF : 2 * HALF, :] = gram[0:HALF, HALF:]
        sub_copy(c).start()
        stat[clusters + c : clusters + c + 1, 0:HALF] = jnp.sum(
            jnp.where(across == down, corner, 0.0), axis=0, keepdims=True
        )

    def add_sub(c):
        sub_copy(c).wait_recv()
        half_sum[c] = packed[c, pl.ds(pl.multiple_of(sub * half, 8), half), :] + sub_in[c]
        for step in range(1, n_samp):
            samp_copy(c, step).start()

    def add_samp(c):
        for step in range(1, n_samp):
            samp_copy(c, step).wait_recv()
        total = half_sum[c, pl.ds(pl.multiple_of(samp * piece, 8), piece), :]
        for step in range(1, n_samp):
            total = total + samp_in[c, step - 1]
        reduced[c] = total

        @pl.when(row != c)
        def _():
            rows_copy(c, row).start()

    def stat_stage(stage):
        if stage == 1:
            stat_sub.wait_recv()
            stat_half[...] = stat[...] + stat_sub_in[...]
            for copy in stat_samp:
                copy.start()
            stat_samp_in[samp] = stat_half[...]
        if stage == 2:
            for copy in stat_samp:
                copy.wait_recv()
            total = stat_samp_in[0]
            for index in range(1, n_samp):
                total = total + stat_samp_in[index]
            stat_rows[row] = total
            for copy in stat_row:
                copy.start()
        if stage == 3:
            for copy in stat_row:
                copy.wait_recv()
            total = stat_rows[0]
            for index in range(1, n_rows):
                total = total + stat_rows[index]
            stat[...] = total

    order = sorted(range(clusters), key=lambda c: -abs(2 * c - clusters + 1))
    for tick in range(clusters + 2):
        if tick < clusters:
            compute(order[tick])
        if tick == clusters - 1:
            stat_sub.start()
        if 0 <= tick - 1 < clusters:
            add_sub(order[tick - 1])
        if tick == clusters:
            stat_stage(1)
        if 0 <= tick - 2 < clusters:
            add_samp(order[tick - 2])
        if tick == clusters + 1:
            stat_stage(2)

    wide[...] = jnp.zeros_like(wide)
    means[...] = jnp.zeros_like(means)
    total = reduced[row]
    for step in range(1, n_rows):
        source = other(row, step, n_rows)
        pltpu.make_async_remote_copy(
            src_ref=rows_in.at[source], dst_ref=rows_in.at[source],
            send_sem=s_rows.at[source], recv_sem=r_rows.at[source],
            device_id={"rows": source}, device_id_type=pl.DeviceIdType.MESH,
        ).wait_recv()
        total = total + rows_in[source]
    gathered[place] = total
    gather = [
        send(
            gathered.at[place], gathered.at[place], s_gat.at[step - 1], r_gat.at[step - 1],
            mate(step),
        )
        for step in range(1, team)
    ]
    for copy in gather:
        copy.start()

    stat_sub.wait_send()
    stat_stage(3)
    centers = stat[0:clusters, :] / stat[clusters : 2 * clusters, features - 1 :]
    means[0:clusters, :] = centers
    own = means[pl.ds(row, 1), :]
    own_line = stat[pl.ds(clusters + row, 1), :]
    own_count = own_line[:, HALF:]
    means_ref[...] = own
    every = means[...]
    top = every.astype(BF16)
    rest = every - top.astype(F32)
    middle = rest.astype(BF16)
    last = (rest - middle.astype(F32)).astype(BF16)
    parts = jnp.concatenate([top, middle, last], axis=0)
    norm = jnp.sum(every * every, axis=1, keepdims=True)
    for start in range(0, rows_total, block):
        span = slice(start, start + block)
        cross = lax.dot_general(parts, scaled[span, :], NT, preferred_element_type=F32)
        cross = cross[0:padded] + (cross[padded : 2 * padded] + cross[2 * padded :])
        distance[:, span] = square[:, span] - 2.0 * cross + norm

    for copy in gather:
        copy.wait_recv()
    whole = gathered[...].reshape(2 * HALF, HALF)
    shared, side = whole[0:HALF], whole[HALF:]
    turned = shared.T
    diagonal = own_line[:, 0:HALF]
    corner = jnp.where(across > down, shared, turned)
    cov[0:HALF, 0:HALF] = jnp.where(across == down, diagonal, corner)
    cov[0:HALF, HALF:] = side
    cov[HALF:, 0:HALF] = side.T
    cov[HALF:, HALF:] = jnp.where(across > down, turned, shared)

    basis = old_ref[...].astype(F32)
    inverse = 1.0 / jnp.concatenate([own_count, own_count], axis=1)
    lane = lax.broadcasted_iota(jnp.int32, (rank, 128), 1)
    line = lax.broadcasted_iota(jnp.int32, (rank, 128), 0)
    for _ in range(STEPS):
        mapped = jnp.dot(basis, cov[...], precision=HIGH, preferred_element_type=F32) * inverse
        mapped = mapped - jnp.sum(basis * own, axis=1, keepdims=True) * own
        wide[rank : 2 * rank, :] = mapped
        table = lax.dot_general(
            mapped, wide[rank : rank + 128, :], NT, precision=HIGH, preferred_element_type=F32
        )
        table = jnp.where(lane == line + rank, 1.0, table)
        for base in range(0, rank, GROUP):
            columns = [
                jnp.broadcast_to(table[:, base + i : base + i + 1], (rank, 128))
                for i in range(GROUP)
            ]
            for i in range(GROUP):
                j = base + i
                inverse_pivot = 1.0 / columns[i][j : j + 1, :]
                factor = jnp.where(line > j, columns[i], 0.0)
                table = table - factor * (table[j : j + 1, :] * inverse_pivot)
                for k in range(i + 1, GROUP):
                    columns[k] = columns[k] - factor * (columns[k][j : j + 1, :] * inverse_pivot)
        diagonal = jnp.sum(jnp.where(lane == line, table, 0.0), axis=1, keepdims=True)
        table = jnp.where(lane < rank, 0.0, table * lax.rsqrt(diagonal))
        basis = jnp.dot(table, wide[0:128, :], precision=HIGH, preferred_element_type=F32)
    bases_ref[...] = basis
    sent[row] = basis.astype(BF16)
    spread = [
        send(
            sent.at[row], sent.at[row], s_bas.at[step - 1], r_bas.at[step - 1],
            {"rows": other(row, step, n_rows)},
        )
        for step in range(1, n_rows)
    ]
    for copy in reversed(spread):
        copy.start()
    for copy in spread:
        copy.wait_recv()

    flat = sent[...].reshape(clusters * rank, features)
    shift = [
        jnp.sum(sent[c].astype(F32) * means[c : c + 1, :], axis=1, keepdims=True)
        for c in range(clusters)
    ]
    for start in range(0, rows_total, block):
        span = slice(start, start + block)
        proj = lax.dot_general(flat, scaled[span, :], NT, preferred_element_type=F32)
        for c in range(clusters):
            part = proj[c * rank : (c + 1) * rank] - shift[c]
            value = distance[c : c + 1, span] - jnp.sum(part * part, axis=0, keepdims=True)
            mask = jnp.concatenate(
                [
                    jnp.broadcast_to(pattern_ref[c : c + 1, t : t + 1], (1, TILE))
                    for t in range(start // TILE, (start + block) // TILE)
                ],
                axis=1,
            )
            errors_ref[c : c + 1, span] = mask.astype(F32) * value / features

    for c in range(clusters):
        sub_copy(c).wait_send()
        for step in range(1, n_samp):
            samp_copy(c, step).wait_send()

        @pl.when(row != c)
        def _():
            rows_copy(c, row).wait_send()
    for copy in stat_samp + stat_row + gather + spread:
        copy.wait_send()


def hand_over(n, *refs):
    sources, targets, sems = refs[:n], refs[n : 2 * n], refs[2 * n]
    copies = [pltpu.make_async_copy(sources[i], targets[i], sems.at[i]) for i in range(n)]
    for copy in copies:
        copy.start()
    for copy in copies:
        copy.wait()


def deliver(*arrays):
    n = len(arrays)
    return pl.pallas_call(
        functools.partial(hand_over, n),
        out_shape=tuple(jax.ShapeDtypeStruct(a.shape, a.dtype) for a in arrays),
        in_specs=[pl.BlockSpec(memory_space=pltpu.VMEM)] * n,
        out_specs=(pl.BlockSpec(memory_space=pltpu.HBM),) * n,
        scratch_shapes=[pltpu.SemaphoreType.DMA((n,))],
    )(*arrays)


def shards(points, inv_scale, labels, pattern, old_bases):
    n_rows = lax.axis_size("rows")
    n_samp = lax.axis_size("samp")
    n_sub = lax.axis_size("sub")
    rows_total, features = points.shape
    rank = old_bases.shape[1]
    clusters = n_rows
    half = 2 * HALF // n_sub
    piece = half // n_samp
    team = n_samp * n_sub
    padded = round_up(clusters, 16)
    dma = pltpu.SemaphoreType.DMA
    vmem = pltpu.VMEM
    specs = pl.BlockSpec(memory_space=pltpu.VMEM)
    errors, centers, subspace = pl.pallas_call(
        functools.partial(kernel, n_rows, n_samp, n_sub),
        out_shape=(
            jax.ShapeDtypeStruct((clusters, rows_total), F32),
            jax.ShapeDtypeStruct((1, features), F32),
            jax.ShapeDtypeStruct((rank, features), F32),
        ),
        in_specs=[pl.BlockSpec(memory_space=pl.ANY)] * 5,
        out_specs=(specs,) * 3,
        scratch_shapes=[
            vmem((rows_total, features), BF16),
            vmem((features, rows_total), BF16),
            vmem((clusters, 2 * HALF, HALF), F32),
            vmem((clusters, half, HALF), F32),
            vmem((clusters, half, HALF), F32),
            vmem((clusters, n_samp - 1, piece, HALF), F32),
            vmem((clusters, piece, HALF), F32),
            vmem((n_rows, piece, HALF), F32),
            vmem((team, piece, HALF), F32),
            vmem((2 * clusters, features), F32),
            vmem((2 * clusters, features), F32),
            vmem((2 * clusters, features), F32),
            vmem((n_samp, 2 * clusters, features), F32),
            vmem((n_rows, 2 * clusters, features), F32),
            vmem((padded, features), F32),
            vmem((1, rows_total), F32),
            vmem((padded, rows_total), F32),
            vmem((features, features), F32),
            vmem((rank + 128, features), F32),
            vmem((n_rows, rank, features), BF16),
            vmem((rows_total, features), BF16),
            vmem((1, features), F32),
            vmem((1, rows_total), jnp.int32),
            vmem(pattern.shape, jnp.int32),
            vmem((rank, features), BF16),
            dma((4,)), dma((rows_total // min(512, rows_total),)),
            dma((clusters,)), dma((clusters,)),
            dma((clusters, n_samp - 1)), dma((clusters, n_samp - 1)),
            dma((clusters,)), dma((n_rows,)),
            dma((team - 1,)), dma((team - 1,)),
            dma, dma,
            dma((n_samp - 1,)), dma((n_samp - 1,)),
            dma((n_rows - 1,)), dma((n_rows - 1,)),
            dma((n_rows - 1,)), dma((n_rows - 1,)),
        ],
        compiler_params=pltpu.CompilerParams(
            collective_id=0, has_side_effects=True, vmem_limit_bytes=64 * 1024 * 1024 - 160 * 1024
        ),
    )(
        points,
        inv_scale.reshape(1, features),
        labels.reshape(1, rows_total),
        pattern,
        old_bases[0],
    )
    return deliver(errors, centers, subspace[None])


def solution(mesh):
    return jax.shard_map(
        shards,
        mesh=mesh,
        in_specs=(
            P(("groups", "rows", "samp", "sub"), None),
            P("groups"),
            P(("groups", "rows", "samp", "sub"), None),
            P(None, ("groups", "rows", "samp", "sub")),
            P(("groups", "rows"), None, None),
        ),
        out_specs=(
            P(None, ("groups", "rows", "samp", "sub")),
            P(("groups", "rows"), None),
            P(("groups", "rows"), None, None),
        ),
        check_vma=False,
    )
```

```python
import functools

import jax
import jax.numpy as jnp
from jax import lax
from jax.experimental import pallas as pl
from jax.experimental.pallas import tpu as pltpu
from jax.sharding import PartitionSpec as P

TILE = 128
STEPS = 2
HALF = 128
GROUP = 16
F32 = jnp.float32
BF16 = jnp.bfloat16
HIGH = lax.Precision.HIGHEST
NT = (((1,), (1,)), ((), ()))


def round_up(value, unit):
    return -(-value // unit) * unit


def send(src, dst, send_sem, recv_sem, where):
    return pltpu.make_async_remote_copy(
        src_ref=src,
        dst_ref=dst,
        send_sem=send_sem,
        recv_sem=recv_sem,
        device_id=where,
        device_id_type=pl.DeviceIdType.MESH,
    )


def kernel(
    n_rows, n_samp, n_sub,
    points_hbm, scale_hbm, labels_hbm, pattern_hbm, old_hbm,
    errors_hbm, means_hbm, bases_hbm,
    scaled, flipped, packed, sub_in, half_sum, samp_in, reduced, rows_in, gathered,
    stat, stat_sub_in, stat_half, stat_samp_in, stat_rows, means, square, distance,
    cov, wide, sent,
    points_ref, scale_ref, labels_ref, pattern_ref, old_ref, s_in, s_points,
    errors_ref, means_ref, bases_ref, s_out,
    s_sub, r_sub, s_samp, r_samp, s_rows, r_rows, s_gat, r_gat,
    s_st_sub, r_st_sub, s_st_samp, r_st_samp, s_st_rows, r_st_rows, s_bas, r_bas,
):
    clusters = n_rows
    rows_total, features = points_ref.shape
    rank = old_ref.shape[0]
    half = 2 * HALF // n_sub
    piece = half // n_samp
    team = n_samp * n_sub
    row = lax.axis_index("rows")
    samp = lax.axis_index("samp")
    sub = lax.axis_index("sub")
    place = sub * n_samp + samp

    def mate(step):
        spot = lax.rem(place + step, team)
        return {"samp": lax.rem(spot, n_samp), "sub": lax.div(spot, n_samp)}

    def other(index, step, size):
        return lax.rem(index + step, size)

    barrier = pltpu.get_barrier_semaphore()
    for step in range(1, team):
        pl.semaphore_signal(barrier, inc=1, device_id=mate(step), device_id_type=pl.DeviceIdType.MESH)
    for step in range(1, n_rows):
        pl.semaphore_signal(
            barrier, inc=1, device_id={"rows": other(row, step, n_rows)},
            device_id_type=pl.DeviceIdType.MESH,
        )

    block = min(1024, rows_total)
    loads = [
        pltpu.make_async_copy(
            points_hbm.at[start : start + block], points_ref.at[start : start + block],
            s_points.at[start // block],
        )
        for start in range(0, rows_total, block)
    ]
    extras = [
        pltpu.make_async_copy(source, target, s_in.at[index])
        for index, (source, target) in enumerate(
            (
                (scale_hbm, scale_ref),
                (labels_hbm, labels_ref),
                (pattern_hbm, pattern_ref),
                (old_hbm, old_ref),
            )
        )
    ]
    extras[0].start()
    loads[0].start()
    extras[1].start()
    for copy in loads[1:] + extras[2:]:
        copy.start()
    extras[0].wait()

    for start in range(0, rows_total, block):
        span = slice(start, start + block)
        loads[start // block].wait()
        value = (points_ref[span, :].astype(F32) * scale_ref[...]).astype(BF16)
        scaled[span, :] = value
        turned = value.T
        flipped[:, span] = turned
        full = turned.astype(F32)
        square[:, span] = jnp.sum(full * full, axis=0, keepdims=True)

    for copy in extras[1:]:
        copy.wait()
    padded = means.shape[0]
    labels = labels_ref[...]
    member = (
        lax.broadcasted_iota(jnp.int32, (padded, rows_total), 0) == labels
    ).astype(F32)
    sums = jnp.dot(member.astype(BF16), scaled[...], preferred_element_type=F32)
    counts = jnp.broadcast_to(jnp.sum(member, axis=1, keepdims=True), (padded, features))
    stat[0:clusters, :] = sums[0:clusters]
    stat[clusters : 2 * clusters, :] = counts[0:clusters]

    pl.semaphore_wait(barrier, team - 1 + n_rows - 1)
    sub_peer = {"sub": 1 - sub}

    def sub_copy(c):
        return send(
            packed.at[c, pl.ds(pl.multiple_of((1 - sub) * half, 8), half)],
            sub_in.at[c], s_sub.at[c], r_sub.at[c], sub_peer,
        )

    def samp_copy(c, step):
        peer = other(samp, step, n_samp)
        return send(
            half_sum.at[c, pl.ds(pl.multiple_of(peer * piece, 8), piece)],
            samp_in.at[c, step - 1], s_samp.at[c, step - 1], r_samp.at[c, step - 1],
            {"samp": peer},
        )

    def rows_copy(c, source):
        return send(
            reduced.at[c], rows_in.at[source], s_rows.at[c], r_rows.at[source], {"rows": c}
        )

    stat_sub = send(stat, stat_sub_in, s_st_sub, r_st_sub, sub_peer)
    stat_samp = [
        send(
            stat_half, stat_samp_in.at[samp], s_st_samp.at[step - 1], r_st_samp.at[step - 1],
            {"samp": other(samp, step, n_samp)},
        )
        for step in range(1, n_samp)
    ]
    stat_row = [
        send(
            stat_rows.at[row], stat_rows.at[row], s_st_rows.at[step - 1], r_st_rows.at[step - 1],
            {"rows": other(row, step, n_rows)},
        )
        for step in range(1, n_rows)
    ]

    down = lax.broadcasted_iota(jnp.int32, (HALF, HALF), 0)
    across = lax.broadcasted_iota(jnp.int32, (HALF, HALF), 1)

    def compute(c):
        mask = (labels == c).astype(F32).astype(BF16)
        gram = jnp.dot(flipped[...] * mask, scaled[...], preferred_element_type=F32)
        corner, opposite = gram[0:HALF, 0:HALF], gram[HALF:, HALF:]
        packed[c, 0:HALF, :] = jnp.where(across > down, corner, opposite)
        packed[c, HALF : 2 * HALF, :] = gram[0:HALF, HALF:]
        sub_copy(c).start()
        stat[clusters + c : clusters + c + 1, 0:HALF] = jnp.sum(
            jnp.where(across == down, corner, 0.0), axis=0, keepdims=True
        )

    def add_sub(c):
        sub_copy(c).wait_recv()
        half_sum[c] = packed[c, pl.ds(pl.multiple_of(sub * half, 8), half), :] + sub_in[c]
        for step in range(1, n_samp):
            samp_copy(c, step).start()

    def add_samp(c):
        for step in range(1, n_samp):
            samp_copy(c, step).wait_recv()
        total = half_sum[c, pl.ds(pl.multiple_of(samp * piece, 8), piece), :]
        for step in range(1, n_samp):
            total = total + samp_in[c, step - 1]
        reduced[c] = total

        @pl.when(row != c)
        def _():
            rows_copy(c, row).start()

    def stat_stage(stage):
        if stage == 1:
            stat_sub.wait_recv()
            stat_half[...] = stat[...] + stat_sub_in[...]
            for copy in stat_samp:
                copy.start()
            stat_samp_in[samp] = stat_half[...]
        if stage == 2:
            for copy in stat_samp:
                copy.wait_recv()
            total = stat_samp_in[0]
            for index in range(1, n_samp):
                total = total + stat_samp_in[index]
            stat_rows[row] = total
            for copy in stat_row:
                copy.start()
        if stage == 3:
            for copy in stat_row:
                copy.wait_recv()
            total = stat_rows[0]
            for index in range(1, n_rows):
                total = total + stat_rows[index]
            stat[...] = total

    order = sorted(range(clusters), key=lambda c: -abs(2 * c - clusters + 1))
    for tick in range(clusters + 2):
        if tick < clusters:
            compute(order[tick])
        if tick == clusters - 1:
            stat_sub.start()
        if 0 <= tick - 1 < clusters:
            add_sub(order[tick - 1])
        if tick == clusters:
            stat_stage(1)
        if 0 <= tick - 2 < clusters:
            add_samp(order[tick - 2])
        if tick == clusters + 1:
            stat_stage(2)

    wide[...] = jnp.zeros_like(wide)
    means[...] = jnp.zeros_like(means)
    total = reduced[row]
    for step in range(1, n_rows):
        source = other(row, step, n_rows)
        pltpu.make_async_remote_copy(
            src_ref=rows_in.at[source], dst_ref=rows_in.at[source],
            send_sem=s_rows.at[source], recv_sem=r_rows.at[source],
            device_id={"rows": source}, device_id_type=pl.DeviceIdType.MESH,
        ).wait_recv()
        total = total + rows_in[source]
    gathered[place] = total
    gather = [
        send(
            gathered.at[place], gathered.at[place], s_gat.at[step - 1], r_gat.at[step - 1],
            mate(step),
        )
        for step in range(1, team)
    ]
    for copy in gather:
        copy.start()

    stat_sub.wait_send()
    stat_stage(3)
    centers = stat[0:clusters, :] / stat[clusters : 2 * clusters, features - 1 :]
    means[0:clusters, :] = centers
    own = means[pl.ds(row, 1), :]
    own_line = stat[pl.ds(clusters + row, 1), :]
    own_count = own_line[:, HALF:]
    means_ref[...] = own
    every = means[...]
    top = every.astype(BF16)
    rest = every - top.astype(F32)
    middle = rest.astype(BF16)
    last = (rest - middle.astype(F32)).astype(BF16)
    parts = jnp.concatenate([top, middle, last], axis=0)
    norm = jnp.sum(every * every, axis=1, keepdims=True)
    for start in range(0, rows_total, block):
        span = slice(start, start + block)
        cross = lax.dot_general(parts, scaled[span, :], NT, preferred_element_type=F32)
        cross = cross[0:padded] + (cross[padded : 2 * padded] + cross[2 * padded :])
        distance[:, span] = square[:, span] - 2.0 * cross + norm

    for copy in gather:
        copy.wait_recv()
    whole = gathered[...].reshape(2 * HALF, HALF)
    shared, side = whole[0:HALF], whole[HALF:]
    turned = shared.T
    diagonal = own_line[:, 0:HALF]
    corner = jnp.where(across > down, shared, turned)
    cov[0:HALF, 0:HALF] = jnp.where(across == down, diagonal, corner)
    cov[0:HALF, HALF:] = side
    cov[HALF:, 0:HALF] = side.T
    cov[HALF:, HALF:] = jnp.where(across > down, turned, shared)

    basis = old_ref[...].astype(F32)
    inverse = 1.0 / jnp.concatenate([own_count, own_count], axis=1)
    lane = lax.broadcasted_iota(jnp.int32, (rank, 128), 1)
    line = lax.broadcasted_iota(jnp.int32, (rank, 128), 0)
    for _ in range(STEPS):
        mapped = jnp.dot(basis, cov[...], precision=HIGH, preferred_element_type=F32) * inverse
        mapped = mapped - jnp.sum(basis * own, axis=1, keepdims=True) * own
        wide[rank : 2 * rank, :] = mapped
        table = lax.dot_general(
            mapped, wide[rank : rank + 128, :], NT, precision=HIGH, preferred_element_type=F32
        )
        table = jnp.where(lane == line + rank, 1.0, table)
        for base in range(0, rank, GROUP):
            columns = [
                jnp.broadcast_to(table[:, base + i : base + i + 1], (rank, 128))
                for i in range(GROUP)
            ]
            for i in range(GROUP):
                j = base + i
                inverse_pivot = 1.0 / columns[i][j : j + 1, :]
                factor = jnp.where(line > j, columns[i], 0.0)
                table = table - factor * (table[j : j + 1, :] * inverse_pivot)
                for k in range(i + 1, GROUP):
                    columns[k] = columns[k] - factor * (columns[k][j : j + 1, :] * inverse_pivot)
        diagonal = jnp.sum(jnp.where(lane == line, table, 0.0), axis=1, keepdims=True)
        table = jnp.where(lane < rank, 0.0, table * lax.rsqrt(diagonal))
        basis = jnp.dot(table, wide[0:128, :], precision=HIGH, preferred_element_type=F32)
    bases_ref[...] = basis
    sent[row] = basis.astype(BF16)
    spread = [
        send(
            sent.at[row], sent.at[row], s_bas.at[step - 1], r_bas.at[step - 1],
            {"rows": other(row, step, n_rows)},
        )
        for step in range(1, n_rows)
    ]
    for copy in reversed(spread):
        copy.start()
    stores = [
        pltpu.make_async_copy(means_ref, means_hbm, s_out.at[0]),
        pltpu.make_async_copy(bases_ref, bases_hbm, s_out.at[1]),
    ]
    for copy in stores:
        copy.start()
    for copy in spread:
        copy.wait_recv()

    flat = sent[...].reshape(clusters * rank, features)
    shift = [
        jnp.sum(sent[c].astype(F32) * means[c : c + 1, :], axis=1, keepdims=True)
        for c in range(clusters)
    ]
    for start in range(0, rows_total, block):
        span = slice(start, start + block)
        proj = lax.dot_general(flat, scaled[span, :], NT, preferred_element_type=F32)
        for c in range(clusters):
            part = proj[c * rank : (c + 1) * rank] - shift[c]
            value = distance[c : c + 1, span] - jnp.sum(part * part, axis=0, keepdims=True)
            mask = jnp.concatenate(
                [
                    jnp.broadcast_to(pattern_ref[c : c + 1, t : t + 1], (1, TILE))
                    for t in range(start // TILE, (start + block) // TILE)
                ],
                axis=1,
            )
            errors_ref[c : c + 1, span] = mask.astype(F32) * value / features
        stores.append(
            pltpu.make_async_copy(
                errors_ref.at[:, span], errors_hbm.at[:, span], s_out.at[2 + start // block]
            )
        )
        stores[-1].start()

    for c in range(clusters):
        sub_copy(c).wait_send()
        for step in range(1, n_samp):
            samp_copy(c, step).wait_send()

        @pl.when(row != c)
        def _():
            rows_copy(c, row).wait_send()
    for copy in stat_samp + stat_row + gather + spread:
        copy.wait_send()
    for copy in stores:
        copy.wait()


def hand_over(n, *refs):
    sources, targets, sems = refs[:n], refs[n : 2 * n], refs[2 * n]
    copies = [pltpu.make_async_copy(sources[i], targets[i], sems.at[i]) for i in range(n)]
    for copy in copies:
        copy.start()
    for copy in copies:
        copy.wait()


def deliver(*arrays):
    n = len(arrays)
    return pl.pallas_call(
        functools.partial(hand_over, n),
        out_shape=tuple(jax.ShapeDtypeStruct(a.shape, a.dtype) for a in arrays),
        in_specs=[pl.BlockSpec(memory_space=pltpu.VMEM)] * n,
        out_specs=(pl.BlockSpec(memory_space=pltpu.HBM),) * n,
        scratch_shapes=[pltpu.SemaphoreType.DMA((n,))],
    )(*arrays)


def shards(points, inv_scale, labels, pattern, old_bases):
    n_rows = lax.axis_size("rows")
    n_samp = lax.axis_size("samp")
    n_sub = lax.axis_size("sub")
    rows_total, features = points.shape
    rank = old_bases.shape[1]
    clusters = n_rows
    half = 2 * HALF // n_sub
    piece = half // n_samp
    team = n_samp * n_sub
    padded = round_up(clusters, 16)
    dma = pltpu.SemaphoreType.DMA
    vmem = pltpu.VMEM
    errors, centers, subspace = pl.pallas_call(
        functools.partial(kernel, n_rows, n_samp, n_sub),
        out_shape=(
            jax.ShapeDtypeStruct((clusters, rows_total), F32),
            jax.ShapeDtypeStruct((1, features), F32),
            jax.ShapeDtypeStruct((rank, features), F32),
        ),
        in_specs=[pl.BlockSpec(memory_space=pl.ANY)] * 5,
        out_specs=(pl.BlockSpec(memory_space=pl.ANY),) * 3,
        scratch_shapes=[
            vmem((rows_total, features), BF16),
            vmem((features, rows_total), BF16),
            vmem((clusters, 2 * HALF, HALF), F32),
            vmem((clusters, half, HALF), F32),
            vmem((clusters, half, HALF), F32),
            vmem((clusters, n_samp - 1, piece, HALF), F32),
            vmem((clusters, piece, HALF), F32),
            vmem((n_rows, piece, HALF), F32),
            vmem((team, piece, HALF), F32),
            vmem((2 * clusters, features), F32),
            vmem((2 * clusters, features), F32),
            vmem((2 * clusters, features), F32),
            vmem((n_samp, 2 * clusters, features), F32),
            vmem((n_rows, 2 * clusters, features), F32),
            vmem((padded, features), F32),
            vmem((1, rows_total), F32),
            vmem((padded, rows_total), F32),
            vmem((features, features), F32),
            vmem((rank + 128, features), F32),
            vmem((n_rows, rank, features), BF16),
            vmem((rows_total, features), BF16),
            vmem((1, features), F32),
            vmem((1, rows_total), jnp.int32),
            vmem(pattern.shape, jnp.int32),
            vmem((rank, features), BF16),
            dma((4,)), dma((rows_total // min(1024, rows_total),)),
            vmem((clusters, rows_total), F32),
            vmem((1, features), F32),
            vmem((rank, features), F32),
            dma((2 + rows_total // min(1024, rows_total),)),
            dma((clusters,)), dma((clusters,)),
            dma((clusters, n_samp - 1)), dma((clusters, n_samp - 1)),
            dma((clusters,)), dma((n_rows,)),
            dma((team - 1,)), dma((team - 1,)),
            dma, dma,
            dma((n_samp - 1,)), dma((n_samp - 1,)),
            dma((n_rows - 1,)), dma((n_rows - 1,)),
            dma((n_rows - 1,)), dma((n_rows - 1,)),
        ],
        compiler_params=pltpu.CompilerParams(
            collective_id=0, has_side_effects=True, vmem_limit_bytes=64 * 1024 * 1024 - 160 * 1024
        ),
    )(
        points,
        inv_scale.reshape(1, features),
        labels.reshape(1, rows_total),
        pattern,
        old_bases[0],
    )
    return deliver(errors, centers, subspace[None])


def solution(mesh):
    return jax.shard_map(
        shards,
        mesh=mesh,
        in_specs=(
            P(("groups", "rows", "samp", "sub"), None),
            P("groups"),
            P(("groups", "rows", "samp", "sub"), None),
            P(None, ("groups", "rows", "samp", "sub")),
            P(("groups", "rows"), None, None),
        ),
        out_specs=(
            P(None, ("groups", "rows", "samp", "sub")),
            P(("groups", "rows"), None),
            P(("groups", "rows"), None, None),
        ),
        check_vma=False,
    )
```
